32 devices in a mesh: row: 2 (over y), col: 4 (over x, core), tok: 4 (over z).
Axes of the slice: x: 2, y: 2, z: 4, core: 2. Of those that a mesh axis runs over, the one named last changes fastest.
Arguments:
- first_inputs: bfloat16 [1024, 8192], P(('row', 'col'), 'tok'), may hold values from -12 to 12, as said below
- second_inputs: bfloat16 [1024, 8192], P(('row', 'col'), 'tok'), may hold values from -12 to 12, as said below
- first_weights: bfloat16 [8192, 2, 14336], P('tok', None, ('row', 'col')), may hold values from -0.0625 to 0.0625
- second_weights: bfloat16 [8192, 2, 14336], P('tok', None, ('col', 'row')), may hold values from -0.0625 to 0.0625
Outputs:
- unit_scores: float32 [14336, 14336], P(('row', 'tok'), 'col')
The draws below stay inside these ranges and needn't reach their ends.
Inputs may be any that keep to these rules, and one draw needn't show every extreme that they name: `first_inputs`: the first model's layer input for each calibration token. `second_inputs`: the second model's layer input for each calibration token.
All inputs are finite; a program needn't handle non-finite values.
Results may differ from the reference program's by a relative error of at most 0.015.
Values may be sent and summed in bfloat16 or wider, within the bound.
A program may use at most 192 MiB of HBM per device.

```python
import jax
import jax.numpy as jnp
from jax import lax

D = 8192
UNITS_A = 14336
UNITS_B = 14336
TOK_DEV = 256
TOKENS = 1024


def token_rise(lower, upper):
    position = jnp.arange(TOKENS, dtype=jnp.float32)[:, None]
    return lower + (upper - lower) * position / max(TOKENS - 1, 1)


def draw_first_inputs(key, part):
    key = jax.random.fold_in(key, 11)
    key_one = jax.random.fold_in(key, 0)
    key_three = jax.random.fold_in(key, 2)
    common = jax.random.normal(key_three, (1, D), jnp.float32)
    values = jax.random.normal(key_one, (TOKENS, D), jnp.float32) + token_rise(0.4, 1.6) * common
    return jnp.clip(values, -12.0, 12.0).astype(jnp.bfloat16)


def draw_second_inputs(key, part):
    key = jax.random.fold_in(key, 23)
    key_one = jax.random.fold_in(key, 0)
    key_three = jax.random.fold_in(key, 2)
    common = jax.random.normal(key_three, (1, D), jnp.float32)
    values = jax.random.normal(key_one, (TOKENS, D), jnp.float32) + 0.8 * common
    return jnp.clip(values, -12.0, 12.0).astype(jnp.bfloat16)


def steps_of(own_key, dims, shards, low, top_value):
    loudness = 1.0
    for dim, parts in shards:
        steps = jax.random.uniform(jax.random.fold_in(jax.random.fold_in(own_key, 6), dim), (parts,), jnp.float32, low / len(shards), top_value / len(shards))
        loudness = loudness * jnp.repeat(jnp.exp(steps), dims[dim] // parts).reshape((-1,) + (1,) * (len(dims) - 1 - dim))
    return loudness


def bell_draw(own_key, shape, scale, bound, cuts=(), held_as=jnp.bfloat16):
    entries = scale * jax.random.normal(own_key, shape, jnp.float32)
    if cuts:
        entries = entries * steps_of(own_key, shape, cuts, -0.22, 0.18)
    return jnp.clip(entries, -bound, bound).astype(held_as)


def setup_inputs(seed: int = 0) -> dict:
    streams_of = jax.random.split(jax.random.key(seed), 5)
    first_inputs = draw_first_inputs(jax.random.fold_in(streams_of[4], 71), 0)
    second_inputs = draw_second_inputs(jax.random.fold_in(streams_of[4], 71), 0)
    first_weights = bell_draw(streams_of[2], (D, 2, UNITS_A), D ** -0.5, 0.0625, ((0, 4), (2, 8)))
    second_weights = bell_draw(streams_of[3], (D, 2, UNITS_B), D ** -0.5, 0.0625, ((0, 4), (2, 8)))
    return dict(first_inputs=first_inputs, second_inputs=second_inputs, first_weights=first_weights, second_weights=second_weights)


def normalized(inputs, weights):
    gate = jnp.dot(inputs, weights[:, 0, :], preferred_element_type=jnp.float32)
    upward = jnp.dot(inputs, weights[:, 1, :], preferred_element_type=jnp.float32)
    activity = jax.nn.silu(gate) * upward
    center = lax.optimization_barrier(jnp.mean(activity, axis=0))
    deviation = activity - center
    spread = lax.optimization_barrier(jnp.mean(deviation * deviation, axis=0))
    return (deviation * lax.rsqrt(spread + 1e-05)).astype(jnp.bfloat16)

def reference(first_inputs, second_inputs, first_weights, second_weights):
    norm_first = normalized(first_inputs, first_weights)
    norm_second = normalized(second_inputs, second_weights)
    total = jnp.zeros((UNITS_A, UNITS_B), jnp.float32)
    for block in range(TOKENS // TOK_DEV):
        rows_first = norm_first[block * TOK_DEV:(block + 1) * TOK_DEV]
        rows_second = norm_second[block * TOK_DEV:(block + 1) * TOK_DEV]
        partial_term = jnp.dot(rows_first.T, rows_second, preferred_element_type=jnp.float32)
        rounded = lax.optimization_barrier(partial_term.astype(jnp.bfloat16))
        total = total + rounded.astype(jnp.float32)
    return total * float(TOKENS) ** (-0.5)
```

```python
import jax
import jax.numpy as jnp
from jax import lax
from jax.sharding import PartitionSpec as P

HALVES = 2
PIECES = 2
CARRY = jnp.float16


def reduce_to_owner(part, depth):
    me = lax.axis_index("tok")

    def own(d):
        d = jnp.clip(d, 0, depth - 1)
        return lax.dynamic_index_in_dim(part, d, axis=1, keepdims=False).astype(jnp.float32)

    up = down = None
    for step in range(1, depth):
        rise = own(depth - step + me)
        fall = own(step - depth + me)
        if up is not None:
            rise = rise + up.astype(jnp.float32)
            fall = fall + down.astype(jnp.float32)
        up = lax.ppermute(rise.astype(CARRY), "tok", [(i, i + 1) for i in range(step)])
        down = lax.ppermute(
            fall.astype(CARRY), "tok", [(depth - 1 - i, depth - 2 - i) for i in range(step)]
        )
    return own(me) + up.astype(jnp.float32) + down.astype(jnp.float32)


def normalize(summed):
    gate, upward = summed[0], summed[1]
    act = jax.nn.silu(gate) * upward
    inverse = 1.0 / act.shape[1]
    dev = act - jnp.sum(act, axis=1, keepdims=True) * inverse
    spread = jnp.sum(dev * dev, axis=1, keepdims=True) * inverse
    return (dev * lax.rsqrt(spread + 1e-05)).astype(jnp.bfloat16)


def owned_norms(full, weights, half, depth):
    size = weights.shape[2] // HALVES
    part = lax.dot_general(
        weights[:, :, half * size : (half + 1) * size],
        full,
        (((0,), (1,)), ((), ())),
        preferred_element_type=jnp.float32,
    ).astype(CARRY)
    width = size // (depth * PIECES)
    part = part.reshape(2, depth, PIECES, width, full.shape[0])
    return jnp.concatenate(
        [normalize(reduce_to_owner(part[:, :, q], depth)) for q in range(PIECES)], axis=0
    )


def local(first_inputs, second_inputs, first_weights, second_weights):
    depth = lax.axis_size("tok")
    wide = lax.axis_size("col")
    rows = lax.axis_size("row")
    full_second = lax.all_gather(second_inputs, ("row", "col"), axis=0, tiled=True)
    full_first = lax.all_gather(first_inputs, ("row", "col"), axis=0, tiled=True)
    tokens = full_first.shape[0]
    second = []
    for half in range(HALVES):
        norm = owned_norms(full_second, second_weights, half, depth)
        norm = lax.all_gather(norm, ("row", "tok"), axis=0, tiled=True)
        second.append(norm.reshape(rows, -1, tokens))
    second = jnp.concatenate(second, axis=1).reshape(-1, tokens)
    first = []
    for half in range(HALVES):
        norm = owned_norms(full_first, first_weights, half, depth)
        if wide == depth:
            swap = [(c * depth + t, t * depth + c) for c in range(wide) for t in range(depth)]
            norm = lax.ppermute(norm, ("col", "tok"), swap)
            norm = lax.all_gather(norm, "col", axis=0, tiled=True)
        else:
            norm = lax.all_gather(norm, ("col", "tok"), axis=0, tiled=True)
            norm = norm.reshape(wide, -1, tokens)
        first.append(norm)
    if wide == depth:
        first = jnp.concatenate(first, axis=0)
    else:
        first = jnp.concatenate(first, axis=1).reshape(-1, tokens)
        count = first.shape[0] // depth
        first = lax.dynamic_slice_in_dim(first, lax.axis_index("tok") * count, count, axis=0)
    total = lax.dot_general(
        first, second, (((1,), (1,)), ((), ())), preferred_element_type=jnp.float32
    )
    return total * float(tokens) ** (-0.5)


def solution(mesh):
    placed = (
        P(("row", "col"), "tok"),
        P(("row", "col"), "tok"),
        P("tok", None, ("row", "col")),
        P("tok", None, ("col", "row")),
    )
    return jax.shard_map(
        local, mesh=mesh, in_specs=placed, out_specs=P(("row", "tok"), "col"), check_vma=False
    )
```

```python
import functools

import jax
import jax.numpy as jnp
from jax import lax
from jax.sharding import PartitionSpec as P

HALVES = 2
PIECES = 2
WINDOW = 4
CARRY = jnp.float16


def take(part, owner):
    owner = jnp.clip(owner, 0, part.shape[1] - 1)
    return lax.dynamic_index_in_dim(part, owner, axis=1, keepdims=False).astype(jnp.float32)


def reduce_to_owners(makers, depth):
    me = lax.axis_index("tok")
    total = len(makers) * PIECES
    parts, entry = [], []
    held = [None] * total
    order = []
    for slot in range(total + depth - 2):
        for step in range(1, depth):
            piece = slot - step + 1
            if 0 <= piece < total:
                order.append((piece, step))
    for turn, (piece, step) in enumerate(order):
        if piece == len(parts):
            parts += makers[piece // PIECES](entry[piece - PIECES] if piece else None)
        part = parts[piece]
        rise = take(part, depth - step + me)
        fall = take(part, step - depth + me)
        if step > 1:
            rise = rise + held[piece][0].astype(jnp.float32)
            fall = fall + held[piece][1].astype(jnp.float32)
        rise, fall = rise.astype(CARRY), fall.astype(CARRY)
        if turn >= WINDOW:
            before = order[turn - WINDOW][0]
            rise, fall, *held[before] = lax.optimization_barrier((rise, fall, *held[before]))
        held[piece] = [
            lax.ppermute(rise, "tok", [(i, i + 1) for i in range(step)]),
            lax.ppermute(fall, "tok", [(depth - 1 - i, depth - 2 - i) for i in range(step)]),
        ]
        if step == 1:
            entry.append(held[piece][0])
    return [
        take(part, me) + up.astype(jnp.float32) + down.astype(jnp.float32)
        for part, (up, down) in zip(parts, held)
    ]


def gather_line(block, depth):
    ups, downs = [block], [block]
    for step in range(1, depth):
        ups.append(lax.ppermute(ups[-1], "tok", [(i, i + 1) for i in range(step - 1, depth - 1)]))
        downs.append(
            lax.ppermute(downs[-1], "tok", [(i + 1, i) for i in range(depth - step)])
        )
    line = jnp.concatenate(ups[:0:-1] + downs, axis=0)
    size = block.shape[0]
    start = (depth - 1 - lax.axis_index("tok")) * size
    return lax.dynamic_slice_in_dim(line, start, depth * size, axis=0)


def normalize(summed):
    gate, upward = summed[0], summed[1]
    act = jax.nn.silu(gate) * upward
    inverse = 1.0 / act.shape[1]
    dev = act - jnp.sum(act, axis=1, keepdims=True) * inverse
    spread = jnp.sum(dev * dev, axis=1, keepdims=True) * inverse
    return (dev * lax.rsqrt(spread + 1e-05)).astype(jnp.bfloat16)


def partial_sums(full, weights, half, depth, piece_first, after):
    size = weights.shape[2] // HALVES
    width = size // (depth * PIECES)
    tokens = full.shape[0]
    weights = weights[:, :, half * size : (half + 1) * size]
    if after is not None:
        full, _ = lax.optimization_barrier((full, after))
    part = lax.dot_general(
        weights, full, (((0,), (1,)), ((), ())), preferred_element_type=jnp.float32
    ).astype(CARRY)
    if piece_first:
        part = part.reshape(2, PIECES, depth, width, tokens)
        return [part[:, q] for q in range(PIECES)]
    part = part.reshape(2, depth, PIECES, width, tokens)
    return [part[:, :, q] for q in range(PIECES)]


def local(first_inputs, second_inputs, first_weights, second_weights):
    depth = lax.axis_size("tok")
    wide = lax.axis_size("col")
    rows = lax.axis_size("row")
    full_second = lax.all_gather(second_inputs, ("row", "col"), axis=0, tiled=True)
    full_first = lax.all_gather(first_inputs, ("row", "col"), axis=0, tiled=True)
    tokens = full_first.shape[0]
    makers = [
        functools.partial(partial_sums, full, weights, half, depth, piece_first)
        for full, weights, piece_first in (
            (full_second, second_weights, False),
            (full_first, first_weights, True),
        )
        for half in range(HALVES)
    ]
    norms = [normalize(summed) for summed in reduce_to_owners(makers, depth)]
    count = HALVES * PIECES
    second = []
    for half in range(HALVES):
        norm = jnp.concatenate(norms[half * PIECES : (half + 1) * PIECES], axis=0)
        norm = gather_line(norm, depth)
        norm = lax.all_gather(norm, "row", axis=0, tiled=True)
        second.append(norm.reshape(rows, -1, tokens))
    second = jnp.concatenate(second, axis=1).reshape(-1, tokens)
    first = []
    for norm in norms[count:]:
        if wide == depth:
            swap = [(c * depth + t, t * depth + c) for c in range(wide) for t in range(depth)]
            norm = lax.ppermute(norm, ("col", "tok"), swap)
            norm = lax.all_gather(norm, "col", axis=0, tiled=True)
        else:
            norm = lax.all_gather(norm, ("col", "tok"), axis=0, tiled=True)
            norm = norm.reshape(wide, -1, tokens)
        first.append(norm)
    if wide == depth:
        first = jnp.concatenate(first, axis=0)
    else:
        first = jnp.concatenate(first, axis=1).reshape(-1, tokens)
        share = first.shape[0] // depth
        first = lax.dynamic_slice_in_dim(first, lax.axis_index("tok") * share, share, axis=0)
    total = lax.dot_general(
        first, second, (((1,), (1,)), ((), ())), preferred_element_type=jnp.float32
    )
    return total * float(tokens) ** (-0.5)


def solution(mesh):
    placed = (
        P(("row", "col"), "tok"),
        P(("row", "col"), "tok"),
        P("tok", None, ("row", "col")),
        P("tok", None, ("col", "row")),
    )
    return jax.shard_map(
        local, mesh=mesh, in_specs=placed, out_specs=P(("row", "tok"), "col"), check_vma=False
    )
```

```python
import functools

import jax
import jax.numpy as jnp
from jax import lax
from jax.sharding import PartitionSpec as P

HALVES = 2
PIECES = 1
WINDOW = 3
CARRY = jnp.float16


def take(part, owner):
    owner = jnp.clip(owner, 0, part.shape[1] - 1)
    return lax.dynamic_index_in_dim(part, owner, axis=1, keepdims=False).astype(jnp.float32)


def reduce_to_owners(makers, depth):
    me = lax.axis_index("tok")
    total = len(makers) * PIECES
    parts, entry = [], []
    held = [None] * total
    order = []
    for slot in range(total + depth - 2):
        for step in range(1, depth):
            piece = slot - step + 1
            if 0 <= piece < total:
                order.append((piece, step))
    for turn, (piece, step) in enumerate(order):
        if piece == len(parts):
            parts += makers[piece // PIECES](entry[piece - PIECES] if piece else None)
        part = parts[piece]
        rise = take(part, depth - step + me)
        fall = take(part, step - depth + me)
        if step > 1:
            rise = rise + held[piece][0].astype(jnp.float32)
            fall = fall + held[piece][1].astype(jnp.float32)
        rise, fall = rise.astype(CARRY), fall.astype(CARRY)
        if turn >= WINDOW:
            before = order[turn - WINDOW][0]
            rise, fall, *held[before] = lax.optimization_barrier((rise, fall, *held[before]))
        held[piece] = [
            lax.ppermute(rise, "tok", [(i, i + 1) for i in range(step)]),
            lax.ppermute(fall, "tok", [(depth - 1 - i, depth - 2 - i) for i in range(step)]),
        ]
        if step == 1:
            entry.append(held[piece][0])
    return [
        take(part, me) + up.astype(jnp.float32) + down.astype(jnp.float32)
        for part, (up, down) in zip(parts, held)
    ]


def gather_line(block, depth):
    ups, downs = [block], [block]
    for step in range(1, depth):
        ups.append(lax.ppermute(ups[-1], "tok", [(i, i + 1) for i in range(step - 1, depth - 1)]))
        downs.append(
            lax.ppermute(downs[-1], "tok", [(i + 1, i) for i in range(depth - step)])
        )
    line = jnp.concatenate(ups[:0:-1] + downs, axis=0)
    size = block.shape[0]
    start = (depth - 1 - lax.axis_index("tok")) * size
    return lax.dynamic_slice_in_dim(line, start, depth * size, axis=0)


def normalize(summed):
    gate, upward = summed[0], summed[1]
    act = jax.nn.silu(gate) * upward
    inverse = 1.0 / act.shape[1]
    dev = act - jnp.sum(act, axis=1, keepdims=True) * inverse
    spread = jnp.sum(dev * dev, axis=1, keepdims=True) * inverse
    return (dev * lax.rsqrt(spread + 1e-05)).astype(jnp.bfloat16)


def partial_sums(full, weights, half, depth, piece_first, after):
    size = weights.shape[2] // HALVES
    width = size // (depth * PIECES)
    tokens = full.shape[0]
    weights = weights[:, :, half * size : (half + 1) * size]
    if after is not None:
        full, _ = lax.optimization_barrier((full, after))
    part = lax.dot_general(
        weights, full, (((0,), (1,)), ((), ())), preferred_element_type=jnp.float32
    ).astype(CARRY)
    if piece_first:
        part = part.reshape(2, PIECES, depth, width, tokens)
        return [part[:, q] for q in range(PIECES)]
    part = part.reshape(2, depth, PIECES, width, tokens)
    return [part[:, :, q] for q in range(PIECES)]


def local(first_inputs, second_inputs, first_weights, second_weights):
    depth = lax.axis_size("tok")
    wide = lax.axis_size("col")
    rows = lax.axis_size("row")
    full_second = lax.all_gather(second_inputs, ("row", "col"), axis=0, tiled=True)
    full_first = lax.all_gather(first_inputs, ("row", "col"), axis=0, tiled=True)
    tokens = full_first.shape[0]
    makers = [
        functools.partial(partial_sums, full, weights, half, depth, piece_first)
        for full, weights, piece_first in (
            (full_second, second_weights, False),
            (full_first, first_weights, True),
        )
        for half in range(HALVES)
    ]
    norms = [normalize(summed) for summed in reduce_to_owners(makers, depth)]
    count = HALVES * PIECES
    second = []
    for half in range(HALVES):
        norm = jnp.concatenate(norms[half * PIECES : (half + 1) * PIECES], axis=0)
        norm = gather_line(norm, depth)
        norm = lax.all_gather(norm, "row", axis=0, tiled=True)
        second.append(norm.reshape(rows, -1, tokens))
    second = jnp.concatenate(second, axis=1).reshape(-1, tokens)
    first = []
    for norm in norms[count:]:
        if wide == depth:
            swap = [(c * depth + t, t * depth + c) for c in range(wide) for t in range(depth)]
            norm = lax.ppermute(norm, ("col", "tok"), swap)
            norm = lax.all_gather(norm, "col", axis=0, tiled=True)
        else:
            norm = lax.all_gather(norm, ("col", "tok"), axis=0, tiled=True)
            norm = norm.reshape(wide, -1, tokens)
        first.append(norm)
    if wide == depth:
        first = jnp.concatenate(first, axis=0)
    else:
        first = jnp.concatenate(first, axis=1).reshape(-1, tokens)
        share = first.shape[0] // depth
        first = lax.dynamic_slice_in_dim(first, lax.axis_index("tok") * share, share, axis=0)
    total = lax.dot_general(
        first, second, (((1,), (1,)), ((), ())), preferred_element_type=jnp.float32
    )
    return total * float(tokens) ** (-0.5)


def solution(mesh):
    placed = (
        P(("row", "col"), "tok"),
        P(("row", "col"), "tok"),
        P("tok", None, ("row", "col")),
        P("tok", None, ("col", "row")),
    )
    return jax.shard_map(
        local, mesh=mesh, in_specs=placed, out_specs=P(("row", "tok"), "col"), check_vma=False
    )
```
